32 devices in a mesh: freq: 16 (over z, x, core), rec: 2 (over y).
Axes of the slice: x: 2, y: 2, z: 4, core: 2. Of those that a mesh axis runs over, the one named last changes fastest.
Arguments:
- kernel: bfloat16 [2, 64, 256, 9216], P(None, 'freq', None, 'rec'), may hold values from -0.09375 to 0.09375
- focusing_in: bfloat16 [32, 9216, 1024], P('freq', 'rec'), may hold values from -6 to 6
- onset_src: int32 [32, 256], P('freq'), may hold values from 128 to 895
- onset_rec: int32 [32, 9216], P('freq', 'rec'), may hold values from 128 to 895
Outputs:
- focusing: bfloat16 [32, 9216, 1024], P('freq', 'rec')
- upgoing_field: bfloat16 [32, 256, 1024], P('freq', 'rec')
The draws below stay inside these ranges and needn't reach their ends.
All inputs are finite; a program needn't handle non-finite values.
Results may differ from the reference program's by a relative error of at most 0.018.
Values may be sent and summed in bfloat16 or wider, within the bound.
A program may use at most 128 MiB of HBM per device.

```python
import jax
import jax.numpy as jnp
from jax import lax

NR = 9216
S = 256
TRACE_SAMPLES = 1024
LOW = 8
ITERS = 2
NF = 64
FOCAL_POINTS = 32


def plant(result, own_key, smallest, high):
    longest = result.shape.index(max(result.shape))
    spots = []
    for shift in (0, 1):
        where = [jax.random.randint(jax.random.fold_in(own_key, axis), (), 0, length) for axis, length in enumerate(result.shape)]
        where[longest] = (where[longest] + shift) % result.shape[longest]
        spots.append(tuple(where))
    return result.at[spots[0]].set(smallest).at[spots[1]].set(high)


def with_spikes(values, rng, source, target, shards_of, factor):
    def block_of(position):
        return (jnp.arange(values.shape[position]) // (values.shape[position] // shards_of)).reshape((-1,) + (1,) * (values.ndim - 1 - position))

    first = jax.random.permutation(rng, shards_of)[block_of(target)]
    other_side = (block_of(target) + shards_of // 2) % shards_of
    return jnp.where((block_of(source) == first) | (block_of(source) == other_side), factor * values, values)


def block_levels(stream_key, dims, shards, low, largest):
    factor_of = 1.0
    for position, shards_of in shards:
        heights = jax.random.uniform(jax.random.fold_in(jax.random.fold_in(stream_key, 6), position), (shards_of,), jnp.float32, low / len(shards), largest / len(shards))
        factor_of = factor_of * jnp.repeat(jnp.exp(heights), dims[position] // shards_of).reshape((-1,) + (1,) * (len(dims) - 1 - position))
    return factor_of


def gaussian(stream_key, shape, width, bound, shards=(), dtype=jnp.bfloat16):
    result = jax.random.normal(stream_key, shape, jnp.float32) * width
    if len(shards) > 0:
        result = block_levels(stream_key, shape, shards, -0.22, 0.18) * result
    return jnp.clip(result, min=-bound, max=bound).astype(dtype)


def bell_draw_with(stream_key, shape, deviation, limit, shards, heavy, kind=jnp.bfloat16):
    values = deviation * jax.random.normal(stream_key, shape, jnp.float32)
    if shards:
        values = values * block_levels(stream_key, shape, shards, -0.22, 0.18)
    return jnp.clip(with_spikes(values, jax.random.fold_in(stream_key, 3), *heavy), -limit, limit).astype(kind)


def setup_inputs(seed: int = 0) -> dict:
    streams_of = jax.random.split(jax.random.key(seed), 5)
    return {
        "kernel": bell_draw_with(streams_of[0], (2, NF, S, NR), NR ** -0.5, 0.09375, ((1, 16), (3, 2)), (3, 2, 2, 2.0)),
        "focusing_in": gaussian(streams_of[1], (FOCAL_POINTS, NR, TRACE_SAMPLES), 1.0, 6.0, ((0, 16), (1, 2))),
        "onset_src": plant(jax.random.randint(streams_of[2], (FOCAL_POINTS, S), TRACE_SAMPLES // 8, 7 * TRACE_SAMPLES // 8), jax.random.fold_in(streams_of[2], 1), TRACE_SAMPLES // 8, (7 * TRACE_SAMPLES // 8) - 1).astype(jnp.int32),
        "onset_rec": plant(jax.random.randint(streams_of[3], (FOCAL_POINTS, NR), TRACE_SAMPLES // 8, 7 * TRACE_SAMPLES // 8), jax.random.fold_in(streams_of[3], 1), TRACE_SAMPLES // 8, (7 * TRACE_SAMPLES // 8) - 1).astype(jnp.int32),
    }


def make_tables(count, samples, lowest):
    freqs = (lax.iota(jnp.int32, count) + lowest)[:, None]
    times = lax.iota(jnp.int32, samples)[None, :]
    phase = ((freqs * times) % samples).astype(jnp.float32) * (2.0 * 3.141592653589793 / samples)
    both = jnp.stack([jnp.cos(phase), -jnp.sin(phase)])
    forward = both.astype(jnp.bfloat16)
    inverse = (forward.astype(jnp.float32) * (2.0 / samples)).astype(jnp.bfloat16)
    return forward, inverse


def reference(kernel, focusing_in, onset_src, onset_rec):
    band = kernel.shape[1]
    samples = focusing_in.shape[2]
    forward, inverse = make_tables(band, samples, LOW)
    fwd_full = forward.astype(jnp.float32)
    inv_full = inverse.astype(jnp.float32)
    times = lax.iota(jnp.int32, samples)
    keep_src = times[None, None, :] < onset_src[:, :, None]
    keep_rec = times[None, None, :] < onset_rec[:, :, None]
    kernel_spectral = jnp.moveaxis(kernel, 1, 0)

    def forward_one(pair):
        block_slice, spec = pair
        b0 = block_slice[0].astype(jnp.float32)
        b1 = block_slice[1].astype(jnp.float32)
        s0 = spec[0].astype(jnp.float32)
        s1 = spec[1].astype(jnp.float32)
        real = jnp.dot(b0, s0.T, preferred_element_type=jnp.float32) - jnp.dot(b1, s1.T, preferred_element_type=jnp.float32)
        imag = jnp.dot(b0, s1.T, preferred_element_type=jnp.float32) + jnp.dot(b1, s0.T, preferred_element_type=jnp.float32)
        return jnp.stack([real, imag])

    def adjoint_one(pair):
        block_slice, spec = pair
        b0 = block_slice[0].astype(jnp.float32)
        b1 = block_slice[1].astype(jnp.float32)
        h0 = spec[0].astype(jnp.float32)
        h1 = spec[1].astype(jnp.float32)
        real = jnp.dot(b0.T, h0, preferred_element_type=jnp.float32) + jnp.dot(b1.T, h1, preferred_element_type=jnp.float32)
        imag = jnp.dot(b0.T, h1, preferred_element_type=jnp.float32) - jnp.dot(b1.T, h0, preferred_element_type=jnp.float32)
        return jnp.stack([real, imag])

    focusing = focusing_in
    upgoing_field = None
    for step in range(ITERS):
        spectrum = jnp.einsum("prt,ckt->kcpr", focusing.astype(jnp.float32), fwd_full).astype(jnp.bfloat16)
        sums = lax.map(forward_one, (kernel_spectral, spectrum)).astype(jnp.bfloat16)
        signal = jnp.einsum("kcsp,ckt->pst", sums.astype(jnp.float32), inv_full)
        upgoing_field = signal.astype(jnp.bfloat16)
        muted = jnp.where(keep_src, signal, jnp.float32(0.0)).astype(jnp.bfloat16)
        echo = jnp.einsum("pst,ckt->kcsp", muted.astype(jnp.float32), fwd_full).astype(jnp.bfloat16)
        reflected = lax.map(adjoint_one, (kernel_spectral, echo)).astype(jnp.bfloat16)
        update = jnp.einsum("kcrp,ckt->prt", reflected.astype(jnp.float32), inv_full)
        focusing = (focusing_in.astype(jnp.float32) + jnp.where(keep_rec, update, jnp.float32(0.0))).astype(jnp.bfloat16)
    return (focusing, upgoing_field)
```

```python
import functools

import jax
import jax.numpy as jnp
import ml_dtypes
import numpy as np
from jax import lax
from jax.experimental import pallas as pl
from jax.experimental.pallas import tpu as pltpu
from jax.sharding import PartitionSpec as P

LOW = 8
ITERS = 2
MESH = pl.DeviceIdType.MESH
BF16 = jnp.bfloat16
F32 = jnp.float32


def make_tables(count, samples, lowest, points, per):
    freqs = (np.arange(count, dtype=np.int64) + lowest)[:, None]
    times = np.arange(samples, dtype=np.int64)[None, :]
    phase = (freqs * times % samples).astype(np.float32) * np.float32(2.0 * np.pi / samples)
    phase = phase.astype(np.float64)
    both = np.stack([np.cos(phase), -np.sin(phase)]).astype(np.float32).astype(ml_dtypes.bfloat16)
    both = both.astype(np.float32)
    owners = count // per
    rows = both.reshape(2, owners, per, samples).transpose(1, 2, 0, 3)
    full = np.zeros((points, owners, points, per, 2, samples), np.float32)
    for p in range(points):
        full[p, :, p] = rows
    full = full.reshape(points, owners * points * per * 2, samples)
    forward = full.astype(ml_dtypes.bfloat16)
    inverse = (full * np.float32(2.0 / samples)).astype(ml_dtypes.bfloat16)
    return forward, inverse


def pick(length, sizes):
    for size in sizes:
        if length % size == 0:
            return size
    return length


def dot_nt(a, b):
    return lax.dot_general(a, b, (((1,), (1,)), ((), ())), preferred_element_type=F32)


def dot_tn(a, b):
    return lax.dot_general(a, b, (((0,), (0,)), ((), ())), preferred_element_type=F32)


def exchange(me, count, src, dst, ssem, rsem):
    dst[me] = src[me]

    @pl.loop(1, count)
    def _(d):
        peer = lax.rem(me + d, count)
        pltpu.make_async_remote_copy(
            src_ref=src.at[peer],
            dst_ref=dst.at[me],
            send_sem=ssem,
            recv_sem=rsem,
            device_id={"freq": peer},
            device_id_type=MESH,
        ).start()


def settle(count, ref, sem):
    part = ref.at[pl.ds(0, count - 1)]
    pltpu.make_async_copy(part, part, sem).wait()


def mega(
    nf, nr, per, points, chunk, sub,
    kern, fin, ons_rec, ons_src, fwd, inv,
    outq, upgoing,
    kv, send_s, recv_s, send_q, recv_q, finbuf, acc, hmat, gp_send, gp_recv, g_send, g_recv, h_send, h_recv, field,
    ksem, fsem, ss_s, rs_s, ss_q, rs_q, ss_p, rs_p, ss_g, rs_g, ss_h, rs_h, osem,
):
    me = lax.axis_index("freq")
    mr = lax.axis_index("rec")
    chunks, rows, width = kv.shape
    sources = acc.shape[1]
    lanes = acc.shape[2]
    samples = fin.shape[2]
    share = upgoing.shape[1]
    block = lanes // nf
    halves = rows // sources
    times = lax.broadcasted_iota(jnp.int32, (1, samples), 1)

    def kload(ch):
        return pltpu.make_async_copy(
            kern.at[:, pl.ds(pl.multiple_of(ch * chunk, chunk), chunk)], kv.at[ch], ksem.at[ch]
        )

    def fload(ch, slot):
        return pltpu.make_async_copy(
            fin.at[:, pl.ds(pl.multiple_of(ch * chunk, chunk), chunk), :], finbuf.at[slot], fsem.at[slot]
        )

    def prefetch():
        for slot in range(min(2, chunks)):
            fload(slot, slot).start()

    def after(ch, slot):
        @pl.when(ch + 2 < chunks)
        def _():
            fload(ch + 2, slot).start()

    prefetch()
    for ch in range(chunks):
        kload(ch).start()

    barrier = pltpu.get_barrier_semaphore()

    @pl.loop(1, nf)
    def _(d):
        pl.semaphore_signal(barrier, inc=1, device_id={"freq": lax.rem(me + d, nf)}, device_id_type=MESH)

    @pl.loop(1, nr)
    def _(d):
        pl.semaphore_signal(barrier, inc=1, device_id={"rec": lax.rem(mr + d, nr)}, device_id_type=MESH)

    pl.semaphore_wait(barrier, nf - 1 + nr - 1)

    @pl.loop(0, chunks)
    def _(ch):
        slot = lax.rem(ch, 2)
        fload(ch, slot).wait()

        @pl.loop(0, chunk // sub)
        def _(i):
            at = pl.ds(pl.multiple_of(i * sub, sub), sub)
            spec = dot_nt(fwd[0], finbuf[slot, 0, at, :])
            for p in range(1, points):
                spec += dot_nt(fwd[p], finbuf[slot, p, at, :])
            send_s[ch, :, :, at] = spec.astype(BF16).reshape(nf, block, sub)

        after(ch, slot)
        exchange(me, nf, send_s.at[ch], recv_s.at[ch], ss_s.at[ch], rs_s.at[ch])

    for it in range(ITERS):
        last = it == ITERS - 1
        if not last:
            prefetch()
        acc[...] = jnp.zeros_like(acc)

        @pl.loop(0, chunks)
        def _(ch):
            if it == 0:
                kload(ch).wait()
            settle(nf, recv_s.at[ch], rs_s.at[ch])
            settle(nf, send_s.at[ch], ss_s.at[ch])

            @pl.loop(0, halves)
            def _(j):
                at = pl.ds(pl.multiple_of(j * sources, sources), sources)
                acc[j] += dot_nt(kv[ch, at, :], recv_s[ch].reshape(lanes, width))

        lane = lax.broadcasted_iota(jnp.int32, (1, lanes), 1)
        imag = lax.rem(lane, 2) == 1
        which = lax.rem(lax.div(lane, 2), per)
        total = jnp.zeros((sources, lanes), F32)
        for k in range(per):
            one = acc[k]
            two = acc[per + k]
            swapped = jnp.where(imag, pltpu.roll(two, 1, 1), -pltpu.roll(two, lanes - 1, 1))
            total = jnp.where(which == k, one + swapped, total)
        gp_send[it] = total.T.astype(BF16)

        def partial(d, slot):
            return pltpu.make_async_remote_copy(
                src_ref=gp_send.at[it],
                dst_ref=gp_recv.at[it, slot],
                send_sem=ss_p.at[it, d - 1],
                recv_sem=rs_p.at[it, slot],
                device_id={"rec": lax.rem(mr + d, nr)},
                device_id_type=MESH,
            )

        for d in range(1, nr):
            partial(d, d - 1).start()
        full = gp_send[it].astype(F32)
        for d in range(1, nr):
            partial(d, d - 1).wait()
            full += gp_recv[it, d - 1].astype(F32)
        g_send[it] = full.astype(BF16).reshape(nf, block, sources)
        exchange(me, nf, g_send.at[it], g_recv.at[it], ss_g.at[it], rs_g.at[it])
        settle(nf, g_recv.at[it], rs_g.at[it])
        settle(nf, g_send.at[it], ss_g.at[it])

        got = g_recv[it].reshape(lanes, sources)
        echo = jnp.zeros((lanes, sources), F32)
        for p in range(points):
            signal = dot_tn(got, inv[p])
            if last:
                field[p] = signal.astype(BF16)
            muted = jnp.where(times < ons_src[:, p : p + 1], signal, 0.0).astype(BF16)
            echo += dot_nt(fwd[p], muted)
        h_send[it] = echo.astype(BF16).reshape(nf, block, sources)
        exchange(me, nf, h_send.at[it], h_recv.at[it], ss_h.at[it], rs_h.at[it])
        if last:
            mine = pl.ds(pl.multiple_of(mr * share, share), share)
            upgoing[...] = field[:, mine, :]
        settle(nf, h_recv.at[it], rs_h.at[it])
        settle(nf, h_send.at[it], ss_h.at[it])

        straight = h_recv[it].reshape(lanes, sources).astype(F32)
        row = lax.broadcasted_iota(jnp.int32, (lanes, 1), 0)
        imag = lax.rem(row, 2) == 1
        which = lax.rem(lax.div(row, 2), per)
        crossed = jnp.where(imag, -pltpu.roll(straight, 1, 0), pltpu.roll(straight, lanes - 1, 0))
        for c, value in enumerate((straight, crossed)):
            for k in range(per):
                at = (c * per + k) * sources
                hmat[:, at : at + sources] = jnp.where(which == k, value, 0.0).astype(BF16)

        @pl.loop(0, chunks)
        def _(ch):
            back = jnp.dot(hmat[...], kv[ch], preferred_element_type=F32)
            send_q[ch] = back.astype(BF16).reshape(nf, block, width)
            exchange(me, nf, send_q.at[ch], recv_q.at[ch], ss_q.at[ch], rs_q.at[ch])

        @pl.loop(0, chunks)
        def _(ch):
            slot = lax.rem(ch, 2)
            settle(nf, recv_q.at[ch], rs_q.at[ch])
            settle(nf, send_q.at[ch], ss_q.at[ch])
            if last:
                pltpu.make_async_copy(recv_q.at[ch], outq.at[ch], osem.at[ch]).start()
            else:
                fload(ch, slot).wait()

                @pl.loop(0, chunk // sub)
                def _(i):
                    at = pl.ds(pl.multiple_of(i * sub, sub), sub)
                    there = pl.ds(pl.multiple_of(ch * chunk + i * sub, sub), sub)
                    arrived = recv_q[ch, :, :, at].reshape(lanes, sub)
                    spec = jnp.zeros((lanes, sub), F32)
                    for p in range(points):
                        update = dot_tn(arrived, inv[p])
                        kept = jnp.where(times < ons_rec[there, p : p + 1], update, 0.0)
                        focus = (finbuf[slot, p, at, :].astype(F32) + kept).astype(BF16)
                        spec += dot_nt(fwd[p], focus)
                    send_s[ch, :, :, at] = spec.astype(BF16).reshape(nf, block, sub)

                after(ch, slot)
                exchange(me, nf, send_s.at[ch], recv_s.at[ch], ss_s.at[ch], rs_s.at[ch])

    @pl.loop(0, chunks)
    def _(ch):
        pltpu.make_async_copy(recv_q.at[ch], outq.at[ch], osem.at[ch]).wait()


def finish(arrived, fin, ons, inv, out):
    got = arrived[0].reshape(inv.shape[1], arrived.shape[3])
    times = lax.broadcasted_iota(jnp.int32, (1, inv.shape[2]), 1)
    for p in range(out.shape[0]):
        update = dot_tn(got, inv[p])
        kept = jnp.where(times < ons[:, p : p + 1], update, 0.0)
        out[p] = (fin[p].astype(F32) + kept).astype(BF16)


def body(kernel, focusing_in, onset_src, onset_rec):
    nf = lax.axis_size("freq")
    nr = lax.axis_size("rec")
    parts, per, sources, receivers = kernel.shape
    points, _, samples = focusing_in.shape
    share = sources // nr
    chunk = pick(receivers, (768, 384, 256, 128))
    sub = pick(chunk, (256, 128))
    chunks = receivers // chunk
    block = points * per * 2
    lanes = nf * block
    rows = parts * per * sources
    forward, inverse = make_tables(per * nf, samples, LOW, points, per)
    forward, inverse = jnp.asarray(forward), jnp.asarray(inverse)
    ons_rec, ons_src = onset_rec.T, onset_src.T
    vmem = pl.BlockSpec(memory_space=pltpu.VMEM)
    anywhere = pl.BlockSpec(memory_space=pl.ANY)
    big = pltpu.VMEM((chunks, nf, block, chunk), BF16)
    small = pltpu.VMEM((ITERS, nf, block, sources), BF16)
    dma = pltpu.SemaphoreType.DMA
    arrived, upgoing = pl.pallas_call(
        functools.partial(mega, nf, nr, per, points, chunk, sub),
        out_shape=(
            jax.ShapeDtypeStruct((chunks, nf, block, chunk), BF16),
            jax.ShapeDtypeStruct((points, share, samples), BF16),
        ),
        in_specs=[anywhere, anywhere, vmem, vmem, vmem, vmem],
        out_specs=(anywhere, vmem),
        scratch_shapes=[
            pltpu.VMEM((chunks, rows, chunk), BF16),
            big, big, big, big,
            pltpu.VMEM((2, points, chunk, samples), BF16),
            pltpu.VMEM((rows // sources, sources, lanes), F32),
            pltpu.VMEM((lanes, rows), BF16),
            pltpu.VMEM((ITERS, lanes, sources), BF16),
            pltpu.VMEM((ITERS, max(nr - 1, 1), lanes, sources), BF16),
            small, small, small, small,
            pltpu.VMEM((points, sources, samples), BF16),
            dma((chunks,)), dma((2,)),
            dma((chunks,)), dma((chunks,)), dma((chunks,)), dma((chunks,)),
            dma((ITERS, max(nr - 1, 1))), dma((ITERS, max(nr - 1, 1))),
            dma((ITERS,)), dma((ITERS,)), dma((ITERS,)), dma((ITERS,)),
            dma((chunks,)),
        ],
        compiler_params=pltpu.CompilerParams(
            collective_id=0, has_side_effects=True, vmem_limit_bytes=60 * 1024 * 1024
        ),
        name="marchenko",
    )(kernel.reshape(rows, receivers), focusing_in, ons_rec, ons_src, forward, inverse)

    per_chunk = chunk // sub
    focusing = pl.pallas_call(
        finish,
        grid=(receivers // sub,),
        out_shape=jax.ShapeDtypeStruct(focusing_in.shape, BF16),
        in_specs=[
            pl.BlockSpec((1, nf, block, sub), lambda i: (i // per_chunk, 0, 0, i % per_chunk)),
            pl.BlockSpec((points, sub, samples), lambda i: (0, i, 0)),
            pl.BlockSpec((sub, points), lambda i: (i, 0)),
            pl.BlockSpec((points, lanes, samples), lambda i: (0, 0, 0)),
        ],
        out_specs=pl.BlockSpec((points, sub, samples), lambda i: (0, i, 0)),
        compiler_params=pltpu.CompilerParams(vmem_limit_bytes=40 * 1024 * 1024),
        name="finish",
    )(arrived, focusing_in, ons_rec, inverse)
    return (focusing, upgoing)


def solution(mesh):
    placed = (
        P(None, "freq", None, "rec"),
        P("freq", "rec", None),
        P("freq", None),
        P("freq", "rec"),
    )
    return jax.shard_map(
        body,
        mesh=mesh,
        in_specs=placed,
        out_specs=(P("freq", "rec", None), P("freq", "rec", None)),
        check_vma=False,
    )
```
